32 devices in a mesh: orb: 8 (over z, core), spx: 4 (over y, x).
Axes of the slice: x: 2, y: 2, z: 4, core: 2. Of those that a mesh axis runs over, the one named last changes fastest.
Arguments:
- weights: float32 [32768], P('orb'), may hold values from 0.25 to 2
- losvd: bfloat16 [32768, 32, 64], P('orb', 'spx'), may hold values from 0 to 0.015625
- occupancy: int32 [256, 32], P('orb', 'spx'), may hold values 0 or 1
- template_of: int32 [32768], P('orb'), may hold values from 0 to 255
- templates: bfloat16 [256, 4160], P('orb'), may hold values from -0.046875 to 0.046875
- observed: float32 [32, 4096], P('spx'), may hold values from -6 to 6
- inv_sigma: float32 [32, 4096], P('spx'), may hold values from 0.5 to 2
Outputs:
- weights_next: float32 [32768], P('orb')
- residual: float32 [32, 4096], P('spx')
The draws below stay inside these ranges and needn't reach their ends.
All inputs are finite; a program needn't handle non-finite values. No bound on the sum of `occupancy` on one device may be relied on, other than what follows from the above.
Results may differ from the reference program's by a relative error of at most 0.0005.
Values may be sent and summed in bfloat16 or wider, within the bound.
A program may use at most 128 MiB of HBM per device.

```python
import math
import jax
import jax.numpy as jnp
from jax import lax

TEMPL = 256
VBINS = 64
WAVE = 4096
OBLK = 128
ITERS = 1
ORBITS = 32768
SPAX = 32
TWAVE = 4160


def set_ends(result, rng, smallest, high):
    shape = result.shape
    place = [jax.random.randint(jax.random.fold_in(rng, axis), (), 0, shape[axis]) for axis in range(len(shape))]
    result = result.at[tuple(place)].set(smallest)
    longest = shape.index(max(shape))
    place[longest] = (place[longest] + 1) % shape[longest]
    return result.at[tuple(place)].set(high)


def shard_levels(rng, extent, shards, smallest, top_value):
    level, own = 1.0, jax.random.fold_in(rng, 6)
    for axis_at, blocks in shards:
        steps = jnp.exp(jax.random.uniform(jax.random.fold_in(own, axis_at), (blocks,), jnp.float32, smallest / len(shards), top_value / len(shards)))
        level = level * jnp.repeat(steps, extent[axis_at] // blocks).reshape([-1 if axis == axis_at else 1 for axis in range(len(extent))])
    return level


def scatter_about(rng, extent, scale, most, shards=(), kind=jnp.bfloat16):
    result = scale * jax.random.normal(rng, extent, jnp.float32)
    if shards:
        result = result * shard_levels(rng, extent, shards, -0.22, 0.18)
    return jnp.clip(result, -most, most).astype(kind)


def setup_inputs(seed: int = 0) -> dict:
    key_list = jax.random.split(jax.random.key(seed), 8)
    return {
        "weights": jnp.clip(jnp.exp(math.log(2.0) - 2.0794415 * jax.random.uniform(key_list[0], (ORBITS,), jnp.float32) ** shard_levels(key_list[0], (ORBITS,), ((0, 8),), -0.2, 0.2)), 0.25, 2.0),
        "losvd": jnp.clip(0.015625 * jax.random.uniform(key_list[1], (ORBITS, SPAX, VBINS), jnp.float32) ** shard_levels(key_list[1], (ORBITS, SPAX, VBINS), ((0, 8), (1, 4)), -0.2, 0.2), 0.0, 0.015625).astype(jnp.bfloat16),
        "occupancy": set_ends((jax.random.randint(key_list[2], (ORBITS // OBLK, SPAX), 0, 4) < 3).astype(jnp.int32), jax.random.fold_in(key_list[2], 1), 0, 1),
        "template_of": set_ends(jax.random.randint(key_list[3], (ORBITS,), 0, TEMPL), jax.random.fold_in(key_list[3], 1), 0, TEMPL - 1).astype(jnp.int32),
        "templates": scatter_about(key_list[4], (TEMPL, TWAVE), (TEMPL * VBINS) ** -0.5, 0.046875, ((0, 8),)),
        "observed": scatter_about(key_list[5], (SPAX, WAVE), 1.0, 6.0, ((0, 4),), jnp.float32),
        "inv_sigma": jnp.clip(jnp.exp(math.log(2.0) - 1.3862944 * jax.random.uniform(key_list[6], (SPAX, WAVE), jnp.float32) ** shard_levels(key_list[6], (SPAX, WAVE), ((0, 4),), -0.2, 0.2)), 0.5, 2.0),
    }


step_size = 0.5


def reference(weights, losvd, occupancy, template_of, templates, observed, inv_sigma):
    block_count = ORBITS // OBLK
    occupied = occupancy.astype(jnp.bfloat16)
    masked = (losvd.reshape(block_count, OBLK, SPAX, VBINS) * occupied[:, None, :, None]).reshape(block_count, OBLK, SPAX * VBINS)
    template_ids = template_of.reshape(block_count, OBLK)
    shift_list = jnp.arange(VBINS, dtype=jnp.int32)
    templates_wide = templates.astype(jnp.float32)

    def mixture_of(rounded):
        def accumulate(running, block_item):
            block_rows, block_ids, block_weights = block_item
            weighted = block_rows.astype(jnp.float32) * block_weights[:, None]
            return running + jax.ops.segment_sum(weighted, block_ids, num_segments=TEMPL), None

        start_sum = jnp.zeros((TEMPL, SPAX * VBINS), jnp.float32)
        summed, _ = lax.scan(accumulate, start_sum, (masked, template_ids, rounded.reshape(block_count, OBLK)))
        return summed.reshape(TEMPL, SPAX, VBINS)

    def model_of(mixture):
        def accumulate(running, shift_index):
            window = lax.dynamic_slice_in_dim(templates_wide, shift_index, WAVE, 1)
            column = lax.dynamic_index_in_dim(mixture, shift_index, 2, keepdims=False)
            return running + jnp.dot(column.T, window, preferred_element_type=jnp.float32, precision=lax.Precision.HIGHEST), None

        model, _ = lax.scan(accumulate, jnp.zeros((SPAX, WAVE), jnp.float32), shift_list)
        return model

    def response_of(scaled):
        def one_shift(unused, shift_index):
            window = lax.dynamic_slice_in_dim(templates, shift_index, WAVE, 1)
            return unused, jnp.dot(window, scaled.T, preferred_element_type=jnp.float32)

        _, stacked = lax.scan(one_shift, jnp.zeros((), jnp.float32), shift_list)
        return jnp.transpose(stacked, (1, 2, 0)).astype(jnp.bfloat16).reshape(TEMPL, SPAX * VBINS)

    def gradient_of(response):
        def one_block(unused, block_item):
            block_rows, block_ids = block_item
            picked = response[block_ids].astype(jnp.float32)
            return unused, jnp.sum(block_rows.astype(jnp.float32) * picked, axis=1)

        _, parts = lax.scan(one_block, jnp.zeros((), jnp.float32), (masked, template_ids))
        return parts.reshape(ORBITS)

    current = weights
    residual = jnp.zeros((SPAX, WAVE), jnp.float32)
    for iteration in range(ITERS):
        rounded = current.astype(jnp.bfloat16).astype(jnp.float32)
        mixture = mixture_of(rounded)
        model = model_of(mixture)
        residual = (model - observed) * inv_sigma
        scaled = (residual * inv_sigma).astype(jnp.bfloat16)
        response = response_of(scaled)
        gradient = gradient_of(response)
        current = jnp.maximum(current - step_size * gradient, 0.0)
    return current, residual
```

```python
import functools
import jax
import jax.numpy as jnp
from jax import lax
from jax.experimental import pallas as pl
from jax.experimental.pallas import tpu as pltpu
from jax.sharding import PartitionSpec as P

step_size = 0.5
MESH = pl.DeviceIdType.MESH
f32, bf16, i32 = jnp.float32, jnp.bfloat16, jnp.int32
NT = (((1,), (1,)), ((), ()))
NN = (((1,), (0,)), ((), ()))
fine = 8


def dot(a, b, dims):
    return lax.dot_general(a, b, dims, preferred_element_type=f32)


def iota(shape, axis):
    return lax.broadcasted_iota(i32, shape, axis)


def kernel(n, m, velocity_bins, block,
           w_ref, lt_hbm, occ_ref, tid_ref, t_ref, obs_ref, inv_ref,
           out_w, out_res,
           lt, part, pair, mixin, hank, model, modelin, resid, table, grads,
           load_sem, pair_sem, mix_send, mix_recv, mod_send, mod_recv, res_send, res_recv,
           tab_send, tab_recv, fwd_send, grad_send, grad_recv):
    chunks, rows, oc = lt.shape
    spaxels, waves = obs_ref.shape
    own, twaves = t_ref.shape
    coarse = velocity_bins // fine
    wide = hank.shape[1]
    total = n * own
    chips = n // 2
    me = lax.axis_index("orb")
    mine = lax.axis_index("spx")
    core, chip = lax.rem(me, 2), lax.div(me, 2)
    sibling = chip * 2 + (1 - core)

    def load(c):
        return pltpu.make_async_copy(
            lt_hbm.at[:, pl.ds(pl.multiple_of(c * oc, oc), oc)], lt.at[c], load_sem.at[c])

    for c in range(chunks):
        load(c).start()

    barrier = pltpu.get_barrier_semaphore()
    for j in range(1, n):
        pl.semaphore_signal(barrier, inc=1, device_id={"orb": lax.rem(me + j, n)}, device_id_type=MESH)
    for j in range(1, m):
        pl.semaphore_signal(barrier, inc=1, device_id={"spx": lax.rem(mine + j, m)}, device_id_type=MESH)

    four = (2, chips, own, oc)
    row_template = ((iota(four, 1) * 2 + iota(four, 0)) * own + iota(four, 2)).reshape(total, oc)
    occupied = occ_ref[...].astype(f32).astype(bf16)
    blocks = occupied.shape[1]
    part[...] = jnp.zeros_like(part)

    def mix(c, carry):
        load(c).wait()
        at = pl.ds(pl.multiple_of(c * oc, oc), oc)
        place = c * oc + iota((blocks, oc), 1) - iota((blocks, oc), 0) * block
        expand = jnp.where((place >= 0) & (place < block), 1.0, 0.0).astype(bf16)
        mask = dot(occupied, expand, NN).astype(bf16)
        for s in range(spaxels):
            band = pl.ds(s * velocity_bins, velocity_bins)
            lt[c, band, :] = lt[c, band, :] * mask[s : s + 1, :]
        weight = w_ref[:, at].astype(bf16).astype(f32)
        assign = jnp.where(row_template == tid_ref[:, at], weight, 0.0).astype(bf16)
        part[...] += dot(assign, lt[c], NT).reshape(part.shape)
        return carry

    lax.fori_loop(0, chunks, mix, 0)

    pl.semaphore_wait(barrier, n - 1 + m - 1)

    swap = pltpu.make_async_remote_copy(
        src_ref=part.at[1 - core], dst_ref=pair, send_sem=pair_sem.at[0], recv_sem=pair_sem.at[1],
        device_id={"orb": sibling}, device_id_type=MESH)
    swap.start()

    padded = jnp.concatenate(
        [t_ref[...].astype(f32), jnp.zeros((own, wide - twaves), f32)], axis=1)
    for q in range(0, coarse, 2):
        pieces = [pltpu.roll(padded, (wide - fine * k) % wide, 1) if k else padded for k in (q, q + 1)]
        hank[pl.ds(q * own, 2 * own), :] = jnp.concatenate(pieces, axis=0).astype(bf16)
    lane = iota((8, rows), 1)
    lane_coarse = lax.div(lax.rem(lane, velocity_bins), fine)
    cube = (fine, spaxels, rows)
    select = jnp.where(
        iota(cube, 1) * velocity_bins + lane_coarse[None, :1, :] * fine + iota(cube, 0) == iota(cube, 2),
        1.0, 0.0).reshape(fine * spaxels, rows).astype(bf16)
    layers = (coarse, own, rows)
    keep = iota(layers, 0) == lane_coarse[None, :1, :]

    swap.wait()
    part[core] = part[core] + pair[...]

    def to_chip(j):
        other = lax.rem(chip + j, chips)
        return pltpu.make_async_remote_copy(
            src_ref=part.at[core, other], dst_ref=mixin.at[chip],
            send_sem=mix_send.at[j], recv_sem=mix_recv.at[chip],
            device_id={"orb": other * 2 + core}, device_id_type=MESH)

    def arrived(ref, sems, source):
        pltpu.make_async_copy(ref.at[source], ref.at[source], sems.at[source]).wait()

    for j in range(1, chips):
        to_chip(j).start()
    mixture = part[core, chip]
    for j in range(1, chips):
        source = lax.rem(chip + j, chips)
        arrived(mixin, mix_recv, source)
        mixture = mixture + mixin[source]

    high = mixture.astype(bf16)
    low = (mixture - high.astype(f32)).astype(bf16)
    columns = []
    for half in (high, low):
        spread = jnp.where(keep, half.astype(f32)[None], 0.0).reshape(coarse * own, rows).astype(bf16)
        columns.append(dot(select, spread, NT))
    both = jnp.concatenate(columns, axis=0).astype(bf16)
    product = dot(both, hank[...], NN)
    tall = fine * spaxels
    product = product[:tall] + product[tall:]
    sums = product[:spaxels]
    for r in range(1, fine):
        sums = sums + pltpu.roll(product[r * spaxels : (r + 1) * spaxels], wide - r, 1)
    span = waves // n
    for d in range(n):
        model[d] = sums[:, d * span : (d + 1) * span]

    def to_owner(j):
        other = lax.rem(me + j, n)
        return pltpu.make_async_remote_copy(
            src_ref=model.at[other], dst_ref=modelin.at[me],
            send_sem=mod_send.at[j], recv_sem=mod_recv.at[me],
            device_id={"orb": other}, device_id_type=MESH)

    def to_all(j):
        other = lax.rem(me + j, n)
        return pltpu.make_async_remote_copy(
            src_ref=resid.at[me], dst_ref=resid.at[me],
            send_sem=res_send.at[j], recv_sem=res_recv.at[me],
            device_id={"orb": other}, device_id_type=MESH)

    for j in range(1, n):
        to_owner(j).start()
    whole = model[me]
    for j in range(1, n):
        source = lax.rem(me + j, n)
        arrived(modelin, mod_recv, source)
        whole = whole + modelin[source]
    at = pl.ds(pl.multiple_of(me * span, span), span)
    resid[me] = (whole - obs_ref[:, at]) * inv_ref[:, at]
    for j in range(1, n):
        to_all(j).start()
    for j in range(1, n):
        arrived(resid, res_recv, lax.rem(me + j, n))
    residual = jnp.concatenate([resid[d] for d in range(n)], axis=1)
    out_res[...] = residual
    scaled = (residual * inv_ref[...]).astype(bf16).astype(f32)
    scaled = jnp.concatenate([scaled, jnp.zeros((spaxels, wide - waves), f32)], axis=1)
    shifted = jnp.concatenate(
        [pltpu.roll(scaled, r, 1) if r else scaled for r in range(fine)], axis=0).astype(bf16)
    response = dot(hank[...], shifted, NT).astype(bf16)
    laid = dot(response, select, NN).reshape(layers)
    table[me] = jnp.sum(jnp.where(keep, laid, 0.0), axis=0).astype(bf16)

    def to_peer(j):
        other = lax.rem(chip + j, chips)
        return pltpu.make_async_remote_copy(
            src_ref=table.at[me], dst_ref=table.at[me],
            send_sem=tab_send.at[j], recv_sem=tab_recv.at[me],
            device_id={"orb": other * 2 + core}, device_id_type=MESH)

    def forward(j):
        source = lax.rem(chip + j, chips) * 2 + core
        return pltpu.make_async_remote_copy(
            src_ref=table.at[source], dst_ref=table.at[source],
            send_sem=fwd_send.at[j], recv_sem=tab_recv.at[source],
            device_id={"orb": sibling}, device_id_type=MESH)

    for j in range(1, chips):
        to_peer(j).start()
    forward(0).start()
    for j in range(1, chips):
        arrived(table, tab_recv, lax.rem(chip + j, chips) * 2 + core)
        forward(j).start()
    for j in range(chips):
        arrived(table, tab_recv, lax.rem(chip + j, chips) * 2 + 1 - core)

    responses = jnp.concatenate([table[d].astype(f32) for d in range(n)], axis=0).astype(bf16)
    shape = (total, oc)

    def grad(c, carry):
        at = pl.ds(pl.multiple_of(c * oc, oc), oc)
        scores = dot(responses, lt[c], NN)
        grads[mine, :, at] = jnp.sum(
            jnp.where(iota(shape, 0) == tid_ref[:, at], scores, 0.0), axis=0, keepdims=True)
        return carry

    lax.fori_loop(0, chunks, grad, 0)

    def to_group(j):
        return pltpu.make_async_remote_copy(
            src_ref=grads.at[mine], dst_ref=grads.at[mine],
            send_sem=grad_send.at[j], recv_sem=grad_recv.at[mine],
            device_id={"spx": lax.rem(mine + j, m)}, device_id_type=MESH)

    for j in range(1, m):
        to_group(j).start()
    for j in range(1, m):
        arrived(grads, grad_recv, lax.rem(mine + j, m))
    gradient = grads[0]
    for i in range(1, m):
        gradient = gradient + grads[i]
    out_w[...] = jnp.maximum(w_ref[...] - step_size * gradient, 0.0)

    for j in range(1, chips):
        to_chip(j).wait_send()
        to_peer(j).wait_send()
    for j in range(chips):
        forward(j).wait_send()
    for j in range(1, n):
        to_owner(j).wait_send()
        to_all(j).wait_send()
    for j in range(1, m):
        to_group(j).wait_send()


def local(weights, losvd, occupancy, template_of, templates, observed, inv_sigma):
    orbits, spaxels, velocity_bins = losvd.shape
    blocks = occupancy.shape[0]
    n, m = lax.axis_size("orb"), lax.axis_size("spx")
    own, twaves = templates.shape
    waves = observed.shape[1]
    rows = spaxels * velocity_bins
    oc = min(512, orbits)
    chunks = orbits // oc
    wide = -(-twaves // 128) * 128
    chips = n // 2
    coarse = velocity_bins // fine
    dma = pltpu.SemaphoreType.DMA
    vmem = pl.BlockSpec(memory_space=pltpu.VMEM)
    out_w, out_res = pl.pallas_call(
        functools.partial(kernel, n, m, velocity_bins, orbits // blocks),
        out_shape=(jax.ShapeDtypeStruct((1, orbits), f32), jax.ShapeDtypeStruct((spaxels, waves), f32)),
        in_specs=[vmem, pl.BlockSpec(memory_space=pl.ANY)] + [vmem] * 5,
        out_specs=(vmem, vmem),
        scratch_shapes=[
            pltpu.VMEM((chunks, rows, oc), bf16),
            pltpu.VMEM((2, chips, own, rows), f32),
            pltpu.VMEM((chips, own, rows), f32),
            pltpu.VMEM((chips, own, rows), f32),
            pltpu.VMEM((coarse * own, wide), bf16),
            pltpu.VMEM((n, spaxels, waves // n), f32),
            pltpu.VMEM((n, spaxels, waves // n), f32),
            pltpu.VMEM((n, spaxels, waves // n), f32),
            pltpu.VMEM((n, own, rows), bf16),
            pltpu.VMEM((m, 1, orbits), f32),
            dma((chunks,)), dma((2,)),
            dma((chips,)), dma((chips,)),
            dma((n,)), dma((n,)), dma((n,)), dma((n,)),
            dma((chips,)), dma((n,)), dma((chips,)),
            dma((m,)), dma((m,)),
        ],
        compiler_params=pltpu.CompilerParams(
            collective_id=0, has_side_effects=True, vmem_limit_bytes=48 * 2**20),
    )(
        weights.reshape(1, orbits),
        jnp.transpose(losvd, (1, 2, 0)).reshape(rows, orbits),
        occupancy.T,
        template_of.reshape(1, orbits),
        templates, observed, inv_sigma,
    )
    return out_w.reshape(orbits), out_res


def solution(mesh):
    placed = (
        P("orb"),
        P("orb", "spx", None),
        P("orb", "spx"),
        P("orb"),
        P("orb", None),
        P("spx", None),
        P("spx", None),
    )
    return jax.shard_map(
        local, mesh=mesh, in_specs=placed, out_specs=(P("orb"), P("spx", None)), check_vma=False
    )
```

```python
import functools
import jax
import jax.numpy as jnp
from jax import lax
from jax.experimental import pallas as pl
from jax.experimental.pallas import tpu as pltpu
from jax.sharding import PartitionSpec as P

step_size = 0.5
MESH = pl.DeviceIdType.MESH
f32, bf16, i32 = jnp.float32, jnp.bfloat16, jnp.int32
NT = (((1,), (1,)), ((), ()))
NN = (((1,), (0,)), ((), ()))
fine = 8


def dot(a, b, dims):
    return lax.dot_general(a, b, dims, preferred_element_type=f32)


def iota(shape, axis):
    return lax.broadcasted_iota(i32, shape, axis)


def kernel(n, m, velocity_bins, block,
           w_hbm, lt_hbm, occ_hbm, tid_hbm, t_hbm, obs_hbm, inv_hbm,
           out_w, out_res,
           w_ref, occ_ref, tid_ref, t_ref, obs_ref, inv_ref,
           lt, masks, assigned, part, pair, mixin, hank, model, modelin, resid, table, grads,
           small_sem, load_sem, pair_send, pair_recv, mix_send, mix_recv, mod_send, mod_recv,
           res_send, res_recv, tab_send, tab_recv, fwd_send, grad_send, grad_recv):
    halves, chunks, rows, oc = lt.shape
    spaxels, waves = obs_ref.shape
    own, twaves = t_ref.shape
    coarse = velocity_bins // fine
    wide = hank.shape[1]
    total = n * own
    chips = n // 2
    span = waves // n
    reach = span + wide - waves
    tall = fine * spaxels
    groups = grads.shape[0]
    me = lax.axis_index("orb")
    mine = lax.axis_index("spx")
    core, chip = lax.rem(me, 2), lax.div(me, 2)
    sibling = chip * 2 + (1 - core)

    def load(h, c):
        return pltpu.make_async_copy(
            lt_hbm.at[pl.ds(h * rows, rows), pl.ds(pl.multiple_of(c * oc, oc), oc)],
            lt.at[h, c], load_sem.at[h, c])

    small = [
        pltpu.make_async_copy(source, target, small_sem.at[i])
        for i, (source, target) in enumerate(
            ((occ_hbm, occ_ref), (tid_hbm, tid_ref), (w_hbm, w_ref),
             (t_hbm, t_ref), (obs_hbm, obs_ref), (inv_hbm, inv_ref)))
    ]
    for copy in small[:3]:
        copy.start()
    for h in range(halves):
        for c in range(chunks):
            load(h, c).start()
    for copy in small[3:]:
        copy.start()

    barrier = pltpu.get_barrier_semaphore()
    for j in range(1, n):
        pl.semaphore_signal(barrier, inc=1, device_id={"orb": lax.rem(me + j, n)}, device_id_type=MESH)
    for j in range(1, m):
        pl.semaphore_signal(barrier, inc=1, device_id={"spx": lax.rem(mine + j, m)}, device_id_type=MESH)

    four = (2, chips, own, oc)
    row_template = ((iota(four, 1) * 2 + iota(four, 0)) * own + iota(four, 2)).reshape(total, oc)
    part[...] = jnp.zeros_like(part)
    for copy in small[:3]:
        copy.wait()
    occupied = occ_ref[...].astype(f32).astype(bf16)
    blocks = occupied.shape[1]

    def cover(h, c, mask):
        for s in range(rows // velocity_bins):
            band = pl.ds(s * velocity_bins, velocity_bins)
            row = h * (rows // velocity_bins) + s
            lt[h, c, band, :] = lt[h, c, band, :] * mask[row : row + 1, :]

    def mix_first(c, carry):
        at = pl.ds(pl.multiple_of(c * oc, oc), oc)
        place = c * oc + iota((blocks, oc), 1) - iota((blocks, oc), 0) * block
        expand = jnp.where((place >= 0) & (place < block), 1.0, 0.0).astype(bf16)
        mask = dot(occupied, expand, NN)
        masks[c] = mask
        weight = w_ref[:, at].astype(bf16).astype(f32)
        assign = jnp.where(row_template == tid_ref[:, at], weight, 0.0).astype(bf16)
        assigned[c] = assign
        load(0, c).wait()
        cover(0, c, mask.astype(bf16))
        part[0] += dot(assign, lt[0, c], NT).reshape(part.shape[1:])
        return carry

    lax.fori_loop(0, chunks, mix_first, 0)

    def swap(h):
        return pltpu.make_async_remote_copy(
            src_ref=part.at[h, 1 - core], dst_ref=pair.at[h],
            send_sem=pair_send.at[h], recv_sem=pair_recv.at[h],
            device_id={"orb": sibling}, device_id_type=MESH)

    def to_chip(h, j):
        other = lax.rem(chip + j, chips)
        return pltpu.make_async_remote_copy(
            src_ref=part.at[h, core, other], dst_ref=mixin.at[h, chip],
            send_sem=mix_send.at[h, j], recv_sem=mix_recv.at[h, chip],
            device_id={"orb": other * 2 + core}, device_id_type=MESH)

    def arrived(ref, sem):
        pltpu.make_async_copy(ref, ref, sem).wait()

    pl.semaphore_wait(barrier, n - 1 + m - 1)
    swap(0).start()

    def mix(h):
        def step(c, carry):
            load(h, c).wait()
            cover(h, c, masks[c].astype(bf16))
            part[h] += dot(assigned[c], lt[h, c], NT).reshape(part.shape[1:])
            return carry

        lax.fori_loop(0, chunks, step, 0)

    def spread(h):
        swap(h).wait()
        part[h, core] = part[h, core] + pair[h]
        for j in range(1, chips):
            to_chip(h, j).start()

    for h in range(1, halves):
        mix(h)
        swap(h).start()
        spread(h - 1)

    for copy in small[3:]:
        copy.wait()
    padded = jnp.concatenate(
        [t_ref[...].astype(f32), jnp.zeros((own, wide - twaves), f32)], axis=1)

    def fold(q):
        pieces = [pltpu.roll(padded, (wide - fine * k) % wide, 1) if k else padded for k in (q, q + 1)]
        hank[pl.ds(q * own, 2 * own), :] = jnp.concatenate(pieces, axis=0).astype(bf16)

    fold(0)
    spread(halves - 1)
    for q in range(2, coarse, 2):
        fold(q)
    lane_coarse = lax.div(lax.rem(iota((8, rows), 1), velocity_bins), fine)
    cube = (fine, spaxels, rows)
    selects = [
        jnp.where(
            (iota(cube, 1) - h * (rows // velocity_bins)) * velocity_bins
            + lane_coarse[None, :1, :] * fine + iota(cube, 0) == iota(cube, 2),
            1.0, 0.0).reshape(tall, rows).astype(bf16)
        for h in range(halves)
    ]
    layers = (coarse, own, rows)
    keep = iota(layers, 0) == lane_coarse[None, :1, :]

    both = None
    for h in range(halves):
        mixture = part[h, core, chip]
        for j in range(1, chips):
            source = lax.rem(chip + j, chips)
            arrived(mixin.at[h, source], mix_recv.at[h, source])
            mixture = mixture + mixin[h, source]
        high = mixture.astype(bf16)
        low = (mixture - high.astype(f32)).astype(bf16)
        columns = []
        for piece in (high, low):
            layered = jnp.where(keep, piece.astype(f32)[None], 0.0).reshape(coarse * own, rows).astype(bf16)
            columns.append(dot(selects[h], layered, NT))
        found = jnp.concatenate(columns, axis=0)
        both = found if both is None else both + found
    both = both.astype(bf16)

    def to_owner(j):
        other = lax.rem(me + j, n)
        return pltpu.make_async_remote_copy(
            src_ref=model.at[other], dst_ref=modelin.at[me],
            send_sem=mod_send.at[j], recv_sem=mod_recv.at[me],
            device_id={"orb": other}, device_id_type=MESH)

    def to_all(j):
        other = lax.rem(me + j, n)
        return pltpu.make_async_remote_copy(
            src_ref=resid.at[me], dst_ref=resid.at[me],
            send_sem=res_send.at[j], recv_sem=res_recv.at[me],
            device_id={"orb": other}, device_id_type=MESH)

    for j in range(1, n + 1):
        other = lax.rem(me + j, n)
        product = dot(both, hank[:, pl.ds(pl.multiple_of(other * span, span), reach)], NN)
        product = product[:tall] + product[tall:]
        sums = product[:spaxels]
        for r in range(1, fine):
            sums = sums + pltpu.roll(product[r * spaxels : (r + 1) * spaxels], reach - r, 1)
        model[other] = sums[:, :span]
        if j < n:
            to_owner(j).start()
    whole = model[me]
    for j in range(1, n):
        source = lax.rem(me + j, n)
        arrived(modelin.at[source], mod_recv.at[source])
        whole = whole + modelin[source]
    at = pl.ds(pl.multiple_of(me * span, span), span)
    resid[me] = (whole - obs_ref[:, at]) * inv_ref[:, at]
    for j in range(1, n):
        to_all(j).start()

    response = jnp.zeros((coarse * own, tall), f32)
    for j in range(n):
        source = lax.rem(me + j, n)
        if j:
            arrived(resid.at[source], res_recv.at[source])
        at = pl.ds(pl.multiple_of(source * span, span), span)
        piece = resid[source]
        out_res[:, at] = piece
        scaled = (piece * inv_ref[:, at]).astype(bf16).astype(f32)
        scaled = jnp.concatenate([scaled, jnp.zeros((spaxels, reach - span), f32)], axis=1)
        shifted = jnp.concatenate(
            [pltpu.roll(scaled, r, 1) if r else scaled for r in range(fine)], axis=0).astype(bf16)
        response = response + dot(
            hank[:, pl.ds(pl.multiple_of(source * span, span), reach)], shifted, NT)
    response = response.astype(bf16)
    for h in range(halves):
        laid = dot(response, selects[h], NN).reshape(layers)
        table[me, :, h * rows : (h + 1) * rows] = jnp.sum(
            jnp.where(keep, laid, 0.0), axis=0).astype(bf16)

    def to_peer(j):
        other = lax.rem(chip + j, chips)
        return pltpu.make_async_remote_copy(
            src_ref=table.at[me], dst_ref=table.at[me],
            send_sem=tab_send.at[j], recv_sem=tab_recv.at[me],
            device_id={"orb": other * 2 + core}, device_id_type=MESH)

    def forward(j):
        source = lax.rem(chip + j, chips) * 2 + core
        return pltpu.make_async_remote_copy(
            src_ref=table.at[source], dst_ref=table.at[source],
            send_sem=fwd_send.at[j], recv_sem=tab_recv.at[source],
            device_id={"orb": sibling}, device_id_type=MESH)

    for j in range(1, chips):
        to_peer(j).start()
    forward(0).start()
    for j in range(1, chips):
        source = lax.rem(chip + j, chips) * 2 + core
        arrived(table.at[source], tab_recv.at[source])
        forward(j).start()
    for j in range(chips):
        source = lax.rem(chip + j, chips) * 2 + 1 - core
        arrived(table.at[source], tab_recv.at[source])

    responses = jnp.concatenate([table[d].astype(f32) for d in range(n)], axis=0).astype(bf16)
    shape = (total, oc)

    def to_group(g, j):
        return pltpu.make_async_remote_copy(
            src_ref=grads.at[g, mine], dst_ref=grads.at[g, mine],
            send_sem=grad_send.at[g, j], recv_sem=grad_recv.at[g, mine],
            device_id={"spx": lax.rem(mine + j, m)}, device_id_type=MESH)

    each = chunks // groups
    for g in range(groups):
        def grad(k, carry, g=g):
            c = g * each + k
            at = pl.ds(pl.multiple_of(c * oc, oc), oc)
            scores = dot(responses[:, :rows], lt[0, c], NN)
            for h in range(1, halves):
                scores = scores + dot(responses[:, h * rows : (h + 1) * rows], lt[h, c], NN)
            grads[g, mine, :, pl.ds(pl.multiple_of(k * oc, oc), oc)] = jnp.sum(
                jnp.where(iota(shape, 0) == tid_ref[:, at], scores, 0.0), axis=0, keepdims=True)
            return carry

        lax.fori_loop(0, each, grad, 0)
        for j in range(1, m):
            to_group(g, j).start()
    for g in range(groups):
        for j in range(1, m):
            source = lax.rem(mine + j, m)
            arrived(grads.at[g, source], grad_recv.at[g, source])
        gradient = grads[g, 0]
        for i in range(1, m):
            gradient = gradient + grads[g, i]
        at = slice(g * each * oc, (g + 1) * each * oc)
        out_w[:, at] = jnp.maximum(w_ref[:, at] - step_size * gradient, 0.0)

    for h in range(halves):
        for j in range(1, chips):
            to_chip(h, j).wait_send()
    for j in range(1, chips):
        to_peer(j).wait_send()
    for j in range(chips):
        forward(j).wait_send()
    for j in range(1, n):
        to_owner(j).wait_send()
        to_all(j).wait_send()
    for g in range(groups):
        for j in range(1, m):
            to_group(g, j).wait_send()


def local(weights, losvd, occupancy, template_of, templates, observed, inv_sigma):
    orbits, spaxels, velocity_bins = losvd.shape
    blocks = occupancy.shape[0]
    n, m = lax.axis_size("orb"), lax.axis_size("spx")
    own, twaves = templates.shape
    waves = observed.shape[1]
    rows = spaxels * velocity_bins
    oc = min(512, orbits)
    chunks = orbits // oc
    wide = waves + -(-(twaves - waves) // 128) * 128
    halves = groups = 2
    half = rows // halves
    chips = n // 2
    coarse = velocity_bins // fine
    dma = pltpu.SemaphoreType.DMA
    vmem = pl.BlockSpec(memory_space=pltpu.VMEM)
    out_w, out_res = pl.pallas_call(
        functools.partial(kernel, n, m, velocity_bins, orbits // blocks),
        out_shape=(jax.ShapeDtypeStruct((1, orbits), f32), jax.ShapeDtypeStruct((spaxels, waves), f32)),
        in_specs=[pl.BlockSpec(memory_space=pltpu.HBM)] * 7,
        out_specs=(vmem, vmem),
        scratch_shapes=[
            pltpu.VMEM((1, orbits), f32),
            pltpu.VMEM((spaxels, blocks), i32),
            pltpu.VMEM((1, orbits), i32),
            pltpu.VMEM((own, twaves), bf16),
            pltpu.VMEM((spaxels, waves), f32),
            pltpu.VMEM((spaxels, waves), f32),
            pltpu.VMEM((halves, chunks, half, oc), bf16),
            pltpu.VMEM((chunks, spaxels, oc), f32),
            pltpu.VMEM((chunks, n * own, oc), bf16),
            pltpu.VMEM((halves, 2, chips, own, half), f32),
            pltpu.VMEM((halves, chips, own, half), f32),
            pltpu.VMEM((halves, chips, own, half), f32),
            pltpu.VMEM((coarse * own, wide), bf16),
            pltpu.VMEM((n, spaxels, waves // n), f32),
            pltpu.VMEM((n, spaxels, waves // n), f32),
            pltpu.VMEM((n, spaxels, waves // n), f32),
            pltpu.VMEM((n, own, rows), bf16),
            pltpu.VMEM((groups, m, 1, orbits // groups), f32),
            dma((6,)), dma((halves, chunks)), dma((halves,)), dma((halves,)),
            dma((halves, chips)), dma((halves, chips)),
            dma((n,)), dma((n,)), dma((n,)), dma((n,)),
            dma((chips,)), dma((n,)), dma((chips,)),
            dma((groups, m)), dma((groups, m)),
        ],
        compiler_params=pltpu.CompilerParams(
            collective_id=0, has_side_effects=True, vmem_limit_bytes=48 * 2**20),
    )(
        weights.reshape(1, orbits),
        jnp.transpose(losvd, (1, 2, 0)).reshape(rows, orbits),
        occupancy.T,
        template_of.reshape(1, orbits),
        templates, observed, inv_sigma,
    )
    return out_w.reshape(orbits), out_res


def solution(mesh):
    placed = (
        P("orb"),
        P("orb", "spx", None),
        P("orb", "spx"),
        P("orb"),
        P("orb", None),
        P("spx", None),
        P("spx", None),
    )
    return jax.shard_map(
        local, mesh=mesh, in_specs=placed, out_specs=(P("orb"), P("spx", None)), check_vma=False
    )
```

```python
import functools
import jax
import jax.numpy as jnp
from jax import lax
from jax.experimental import pallas as pl
from jax.experimental.pallas import tpu as pltpu
from jax.sharding import PartitionSpec as P

step_size = 0.5
MESH = pl.DeviceIdType.MESH
f32, bf16, i32 = jnp.float32, jnp.bfloat16, jnp.int32
NT = (((1,), (1,)), ((), ()))
NN = (((1,), (0,)), ((), ()))
fine = 8


def dot(a, b, dims):
    return lax.dot_general(a, b, dims, preferred_element_type=f32)


def iota(shape, axis):
    return lax.broadcasted_iota(i32, shape, axis)


def kernel(n, m, velocity_bins, block,
           w_hbm, lt_hbm, occ_hbm, tid_hbm, t_hbm, obs_hbm, inv_hbm,
           out_w, out_res,
           w_ref, occ_ref, tid_ref, t_ref, obs_ref, inv_ref,
           lt, masks, assigned, part, pair, mixin, hank, model, modelin, resid, table, grads,
           small_sem, load_sem, pair_send, pair_recv, mix_send, mix_recv, mod_send, mod_recv,
           res_send, res_recv, tab_send, tab_recv, fwd_send, grad_send, grad_recv):
    halves, chunks, rows, oc = lt.shape
    spaxels, waves = obs_ref.shape
    own, twaves = t_ref.shape
    coarse = velocity_bins // fine
    wide = hank.shape[1]
    total = n * own
    chips = n // 2
    span = waves // n
    reach = span + wide - waves
    tall = fine * spaxels
    groups = grads.shape[0]
    me = lax.axis_index("orb")
    mine = lax.axis_index("spx")
    core, chip = lax.rem(me, 2), lax.div(me, 2)
    sibling = chip * 2 + (1 - core)

    def load(h, c):
        return pltpu.make_async_copy(
            lt_hbm.at[pl.ds(h * rows, rows), pl.ds(pl.multiple_of(c * oc, oc), oc)],
            lt.at[h, c], load_sem.at[h, c])

    small = [
        pltpu.make_async_copy(source, target, small_sem.at[i])
        for i, (source, target) in enumerate(
            ((occ_hbm, occ_ref), (tid_hbm, tid_ref), (w_hbm, w_ref),
             (t_hbm, t_ref), (obs_hbm, obs_ref), (inv_hbm, inv_ref)))
    ]
    for copy in small[:3]:
        copy.start()
    for h in range(halves):
        for c in range(chunks):
            load(h, c).start()
    for copy in small[3:]:
        copy.start()

    barrier = pltpu.get_barrier_semaphore()
    for j in range(1, n):
        pl.semaphore_signal(barrier, inc=1, device_id={"orb": lax.rem(me + j, n)}, device_id_type=MESH)
    for j in range(1, m):
        pl.semaphore_signal(barrier, inc=1, device_id={"spx": lax.rem(mine + j, m)}, device_id_type=MESH)

    four = (2, chips, own, oc)
    row_template = ((iota(four, 1) * 2 + iota(four, 0)) * own + iota(four, 2)).reshape(total, oc)
    part[...] = jnp.zeros_like(part)
    for copy in small[:3]:
        copy.wait()
    occupied = occ_ref[...].astype(f32).astype(bf16)
    blocks = occupied.shape[1]

    def cover(h, c, mask):
        for s in range(rows // velocity_bins):
            band = pl.ds(s * velocity_bins, velocity_bins)
            row = h * (rows // velocity_bins) + s
            lt[h, c, band, :] = lt[h, c, band, :] * mask[row : row + 1, :]

    def mix_first(c, carry):
        at = pl.ds(pl.multiple_of(c * oc, oc), oc)
        place = c * oc + iota((blocks, oc), 1) - iota((blocks, oc), 0) * block
        expand = jnp.where((place >= 0) & (place < block), 1.0, 0.0).astype(bf16)
        mask = dot(occupied, expand, NN)
        masks[c] = mask
        weight = w_ref[:, at].astype(bf16).astype(f32)
        assign = jnp.where(row_template == tid_ref[:, at], weight, 0.0).astype(bf16)
        assigned[c] = assign
        load(0, c).wait()
        cover(0, c, mask.astype(bf16))
        part[0] += dot(assign, lt[0, c], NT).reshape(part.shape[1:])
        return carry

    lax.fori_loop(0, chunks, mix_first, 0)

    def swap(h):
        return pltpu.make_async_remote_copy(
            src_ref=part.at[h, 1 - core], dst_ref=pair.at[h],
            send_sem=pair_send.at[h], recv_sem=pair_recv.at[h],
            device_id={"orb": sibling}, device_id_type=MESH)

    def to_chip(h, j):
        other = lax.rem(chip + j, chips)
        return pltpu.make_async_remote_copy(
            src_ref=part.at[h, core, other], dst_ref=mixin.at[h, chip],
            send_sem=mix_send.at[h, j], recv_sem=mix_recv.at[h, chip],
            device_id={"orb": other * 2 + core}, device_id_type=MESH)

    def arrived(ref, sem):
        pltpu.make_async_copy(ref, ref, sem).wait()

    pl.semaphore_wait(barrier, n - 1 + m - 1)
    swap(0).start()

    def mix(h):
        def step(c, carry):
            load(h, c).wait()
            cover(h, c, masks[c].astype(bf16))
            part[h] += dot(assigned[c], lt[h, c], NT).reshape(part.shape[1:])
            return carry

        lax.fori_loop(0, chunks, step, 0)

    def spread(h):
        swap(h).wait()
        part[h, core] = part[h, core] + pair[h]
        for j in range(1, chips):
            to_chip(h, j).start()

    for h in range(1, halves):
        mix(h)
        swap(h).start()
        spread(h - 1)

    for copy in small[3:]:
        copy.wait()
    padded = jnp.concatenate(
        [t_ref[...].astype(f32), jnp.zeros((own, wide - twaves), f32)], axis=1)

    def fold(q):
        pieces = [pltpu.roll(padded, (wide - fine * k) % wide, 1) if k else padded for k in (q, q + 1)]
        hank[pl.ds(q * own, 2 * own), :] = jnp.concatenate(pieces, axis=0).astype(bf16)

    fold(0)
    spread(halves - 1)
    for q in range(2, coarse, 2):
        fold(q)
    lane_coarse = lax.div(lax.rem(iota((8, rows), 1), velocity_bins), fine)
    cube = (fine, spaxels, rows)
    selects = [
        jnp.where(
            (iota(cube, 1) - h * (rows // velocity_bins)) * velocity_bins
            + lane_coarse[None, :1, :] * fine + iota(cube, 0) == iota(cube, 2),
            1.0, 0.0).reshape(tall, rows).astype(bf16)
        for h in range(halves)
    ]
    layers = (coarse, own, rows)
    keep = iota(layers, 0) == lane_coarse[None, :1, :]

    both = None
    for h in range(halves):
        mixture = part[h, core, chip]
        for j in range(1, chips):
            source = lax.rem(chip + j, chips)
            arrived(mixin.at[h, source], mix_recv.at[h, source])
            mixture = mixture + mixin[h, source]
        high = mixture.astype(bf16)
        low = (mixture - high.astype(f32)).astype(bf16)
        columns = []
        for piece in (high, low):
            layered = jnp.where(keep, piece.astype(f32)[None], 0.0).reshape(coarse * own, rows).astype(bf16)
            columns.append(dot(selects[h], layered, NT))
        found = jnp.concatenate(columns, axis=0)
        both = found if both is None else both + found
    both = both.astype(bf16)

    def to_owner(j):
        other = lax.rem(me + j, n)
        return pltpu.make_async_remote_copy(
            src_ref=model.at[other], dst_ref=modelin.at[me],
            send_sem=mod_send.at[j], recv_sem=mod_recv.at[me],
            device_id={"orb": other}, device_id_type=MESH)

    def to_all(j):
        other = lax.rem(me + j, n)
        return pltpu.make_async_remote_copy(
            src_ref=resid.at[me], dst_ref=resid.at[me],
            send_sem=res_send.at[j], recv_sem=res_recv.at[me],
            device_id={"orb": other}, device_id_type=MESH)

    for j in range(1, n + 1):
        other = lax.rem(me + j, n)
        product = dot(both, hank[:, pl.ds(pl.multiple_of(other * span, span), reach)], NN)
        product = product[:tall] + product[tall:]
        sums = product[:spaxels]
        for r in range(1, fine):
            sums = sums + pltpu.roll(product[r * spaxels : (r + 1) * spaxels], reach - r, 1)
        model[other] = sums[:, :span]
        if j < n:
            to_owner(j).start()
    whole = model[me]
    for j in range(1, n):
        source = lax.rem(me + j, n)
        arrived(modelin.at[source], mod_recv.at[source])
        whole = whole + modelin[source]
    at = pl.ds(pl.multiple_of(me * span, span), span)
    resid[me] = (whole - obs_ref[:, at]) * inv_ref[:, at]
    for j in range(1, n):
        to_all(j).start()

    response = jnp.zeros((coarse * own, tall), f32)
    for j in range(n):
        source = lax.rem(me + j, n)
        if j:
            arrived(resid.at[source], res_recv.at[source])
        at = pl.ds(pl.multiple_of(source * span, span), span)
        piece = resid[source]
        out_res[:, at] = piece
        scaled = (piece * inv_ref[:, at]).astype(bf16).astype(f32)
        scaled = jnp.concatenate([scaled, jnp.zeros((spaxels, reach - span), f32)], axis=1)
        shifted = jnp.concatenate(
            [pltpu.roll(scaled, r, 1) if r else scaled for r in range(fine)], axis=0).astype(bf16)
        response = response + dot(
            hank[:, pl.ds(pl.multiple_of(source * span, span), reach)], shifted, NT)
    response = response.astype(bf16)
    for h in range(halves):
        laid = dot(response, selects[h], NN).reshape(layers)
        table[me, :, h * rows : (h + 1) * rows] = jnp.sum(
            jnp.where(keep, laid, 0.0), axis=0).astype(bf16)

    def to_peer(j):
        other = lax.rem(chip + j, chips)
        return pltpu.make_async_remote_copy(
            src_ref=table.at[me], dst_ref=table.at[me],
            send_sem=tab_send.at[j], recv_sem=tab_recv.at[me],
            device_id={"orb": other * 2 + core}, device_id_type=MESH)

    def forward(j):
        source = lax.rem(chip + j, chips) * 2 + core
        return pltpu.make_async_remote_copy(
            src_ref=table.at[source], dst_ref=table.at[source],
            send_sem=fwd_send.at[j], recv_sem=tab_recv.at[source],
            device_id={"orb": sibling}, device_id_type=MESH)

    for j in range(1, chips):
        to_peer(j).start()
    forward(0).start()
    for j in range(1, chips):
        source = lax.rem(chip + j, chips) * 2 + core
        arrived(table.at[source], tab_recv.at[source])
        forward(j).start()
    for j in range(chips):
        source = lax.rem(chip + j, chips) * 2 + 1 - core
        arrived(table.at[source], tab_recv.at[source])

    responses = jnp.concatenate([table[d].astype(f32) for d in range(n)], axis=0).astype(bf16)
    shape = (total, oc)

    def to_group(g, j):
        return pltpu.make_async_remote_copy(
            src_ref=grads.at[g, mine], dst_ref=grads.at[g, mine],
            send_sem=grad_send.at[g, j], recv_sem=grad_recv.at[g, mine],
            device_id={"spx": lax.rem(mine + j, m)}, device_id_type=MESH)

    each = chunks // groups
    for g in range(groups):
        def grad(k, carry, g=g):
            c = g * each + k
            at = pl.ds(pl.multiple_of(c * oc, oc), oc)
            scores = dot(responses[:, :rows], lt[0, c], NN)
            for h in range(1, halves):
                scores = scores + dot(responses[:, h * rows : (h + 1) * rows], lt[h, c], NN)
            grads[g, mine, :, pl.ds(pl.multiple_of(k * oc, oc), oc)] = jnp.sum(
                jnp.where(iota(shape, 0) == tid_ref[:, at], scores, 0.0), axis=0, keepdims=True)
            return carry

        lax.fori_loop(0, each, grad, 0)
        for j in range(1, m):
            to_group(g, j).start()
    for g in range(groups):
        for j in range(1, m):
            source = lax.rem(mine + j, m)
            arrived(grads.at[g, source], grad_recv.at[g, source])
        gradient = grads[g, 0]
        for i in range(1, m):
            gradient = gradient + grads[g, i]
        at = slice(g * each * oc, (g + 1) * each * oc)
        out_w[:, at] = jnp.maximum(w_ref[:, at] - step_size * gradient, 0.0)

    for h in range(halves):
        for j in range(1, chips):
            to_chip(h, j).wait_send()
    for j in range(1, chips):
        to_peer(j).wait_send()
    for j in range(chips):
        forward(j).wait_send()
    for j in range(1, n):
        to_owner(j).wait_send()
        to_all(j).wait_send()
    for g in range(groups):
        for j in range(1, m):
            to_group(g, j).wait_send()


def local(weights, losvd, occupancy, template_of, templates, observed, inv_sigma):
    orbits, spaxels, velocity_bins = losvd.shape
    blocks = occupancy.shape[0]
    n, m = lax.axis_size("orb"), lax.axis_size("spx")
    own, twaves = templates.shape
    waves = observed.shape[1]
    rows = spaxels * velocity_bins
    oc = min(512, orbits)
    chunks = orbits // oc
    wide = waves + -(-(twaves - waves) // 128) * 128
    halves = groups = 1
    half = rows // halves
    chips = n // 2
    coarse = velocity_bins // fine
    dma = pltpu.SemaphoreType.DMA
    vmem = pl.BlockSpec(memory_space=pltpu.VMEM)
    out_w, out_res = pl.pallas_call(
        functools.partial(kernel, n, m, velocity_bins, orbits // blocks),
        out_shape=(jax.ShapeDtypeStruct((1, orbits), f32), jax.ShapeDtypeStruct((spaxels, waves), f32)),
        in_specs=[pl.BlockSpec(memory_space=pltpu.HBM)] * 7,
        out_specs=(vmem, vmem),
        scratch_shapes=[
            pltpu.VMEM((1, orbits), f32),
            pltpu.VMEM((spaxels, blocks), i32),
            pltpu.VMEM((1, orbits), i32),
            pltpu.VMEM((own, twaves), bf16),
            pltpu.VMEM((spaxels, waves), f32),
            pltpu.VMEM((spaxels, waves), f32),
            pltpu.VMEM((halves, chunks, half, oc), bf16),
            pltpu.VMEM((chunks, spaxels, oc), f32),
            pltpu.VMEM((chunks, n * own, oc), bf16),
            pltpu.VMEM((halves, 2, chips, own, half), f32),
            pltpu.VMEM((halves, chips, own, half), f32),
            pltpu.VMEM((halves, chips, own, half), f32),
            pltpu.VMEM((coarse * own, wide), bf16),
            pltpu.VMEM((n, spaxels, waves // n), f32),
            pltpu.VMEM((n, spaxels, waves // n), f32),
            pltpu.VMEM((n, spaxels, waves // n), f32),
            pltpu.VMEM((n, own, rows), bf16),
            pltpu.VMEM((groups, m, 1, orbits // groups), f32),
            dma((6,)), dma((halves, chunks)), dma((halves,)), dma((halves,)),
            dma((halves, chips)), dma((halves, chips)),
            dma((n,)), dma((n,)), dma((n,)), dma((n,)),
            dma((chips,)), dma((n,)), dma((chips,)),
            dma((groups, m)), dma((groups, m)),
        ],
        compiler_params=pltpu.CompilerParams(
            collective_id=0, has_side_effects=True, vmem_limit_bytes=60 * 2**20),
    )(
        weights.reshape(1, orbits),
        jnp.transpose(losvd, (1, 2, 0)).reshape(rows, orbits),
        occupancy.T,
        template_of.reshape(1, orbits),
        templates, observed, inv_sigma,
    )
    return out_w.reshape(orbits), out_res


def solution(mesh):
    placed = (
        P("orb"),
        P("orb", "spx", None),
        P("orb", "spx"),
        P("orb"),
        P("orb", None),
        P("spx", None),
        P("spx", None),
    )
    return jax.shard_map(
        local, mesh=mesh, in_specs=placed, out_specs=(P("orb"), P("spx", None)), check_vma=False
    )
```
